32 devices in a mesh: groups: 2 (over y), occ: 4 (over x, core), vir: 4 (over z).
Axes of the slice: x: 2, y: 2, z: 4, core: 2. Of those that a mesh axis runs over, the one named last changes fastest.
Arguments:
- amps: bfloat16 [16, 256, 8, 256], P(('groups', 'occ'), 'vir'), parts along dimension 0, may hold values from -0.59765625 to 0.59765625
- integrals: bfloat16 [16, 256, 8, 256], P(('groups', 'occ'), 'vir'), parts along dimension 0, may hold values from -0.59765625 to 0.59765625
- ladder_ints: bfloat16 [16, 8, 8, 8], P(('groups', 'occ')), parts along dimension 0, may hold values from -3 to 3
- eps_occ: float32 [16], P('groups'), parts along dimension 0, may hold values from -1 to -0.3
- eps_vir: float32 [512], P('groups'), parts along dimension 0, may hold values from 0.5 to 2
- pair_mask: int32 [16, 8], P(('groups', 'occ')), parts along dimension 0, may hold values 0 or 1
Outputs:
- new_amps: bfloat16 [16, 256, 8, 256], P(('groups', 'occ'), 'vir'), parts along dimension 0
- pair_energy: float32 [16, 8], P(('groups', 'occ')), parts along dimension 0
The draws below stay inside these ranges and needn't reach their ends.
There are 2 independent parts, one for each index of `groups`. The reference program is written for one: setup_inputs(seed, part) draws one part's arguments, and reference() takes and returns one part's arrays. A program takes and returns all parts, laid end to end along the dimension named above; each array names one. Nothing has to cross between parts.
All inputs are finite; a program needn't handle non-finite values. No bound on the sum of `pair_mask` on one device may be relied on, other than what follows from the above.
Results may differ from the reference program's by a relative error of at most 0.00086.
Values may be sent and summed in bfloat16 or wider, within the bound.
A program may use at most 128 MiB of HBM per device.

```python
import jax
import jax.numpy as jnp

O = 8
V = 256


def touch_ends(values, key, low, largest):
    longest = values.shape.index(max(values.shape))
    spots = []
    for shift in (0, 1):
        where = [jax.random.randint(jax.random.fold_in(key, axis), (), 0, length) for axis, length in enumerate(values.shape)]
        where[longest] = (where[longest] + shift) % values.shape[longest]
        spots.append(tuple(where))
    return values.at[spots[0]].set(low).at[spots[1]].set(largest)


def block_scale(key, extent, cuts, low, top_value):
    loudness, own = 1.0, jax.random.fold_in(key, 6)
    for dim, blocks in cuts:
        steps = jnp.exp(jax.random.uniform(jax.random.fold_in(own, dim), (blocks,), jnp.float32, low / len(cuts), top_value / len(cuts)))
        loudness = loudness * jnp.repeat(steps, extent[dim] // blocks).reshape([-1 if axis == dim else 1 for axis in range(len(extent))])
    return loudness


def gaussian(stream_key, extent, width, bound, pieces=(), held_as=jnp.bfloat16):
    result = width * jax.random.normal(stream_key, extent, jnp.float32)
    if pieces:
        result = result * block_scale(stream_key, extent, pieces, -0.22, 0.18)
    return jnp.clip(result, -bound, bound).astype(held_as)


def setup_inputs(seed: int = 0, part: int = 0) -> dict:
    streams_of = jax.random.split(jax.random.key(seed), 7)
    part_keys = jax.random.split(jax.random.fold_in(streams_of[6], part), 7)
    return {
        "amps": gaussian(part_keys[0], (O, V, O, V), 0.1, 0.59765625, ((0, 4), (1, 4))),
        "integrals": gaussian(part_keys[1], (O, V, O, V), 0.1, 0.59765625, ((0, 4), (1, 4))),
        "ladder_ints": gaussian(part_keys[2], (O, O, O, O), (4.0 / O), 3.0, ((0, 4),)),
        "eps_occ": jnp.clip(jax.random.uniform(part_keys[3], (O,), jnp.float32, -1.0, -0.3), -1.0, -0.3),
        "eps_vir": jnp.clip(jax.random.uniform(part_keys[4], (V,), jnp.float32, 0.5, 2.0), 0.5, 2.0),
        "pair_mask": touch_ends((jax.random.randint(part_keys[5], (O, O), 0, 4) < 3).astype(jnp.int32), jax.random.fold_in(part_keys[5], 1), 0, 1),
    }


def reference(amps, integrals, ladder_ints, eps_occ, eps_vir, pair_mask):
    left = integrals.transpose(0, 3, 2, 1).reshape(O * V, O * V)
    right = amps.transpose(0, 3, 2, 1).reshape(O * V, O * V)
    cycle = jnp.dot(left, right, preferred_element_type=jnp.float32)
    cycle = cycle.reshape(O, V, O, V).transpose(0, 3, 2, 1)
    ladder = jnp.einsum("ijkl,kbla->ibja", ladder_ints.astype(jnp.float32), amps.astype(jnp.float32))
    total = integrals.astype(jnp.float32) + cycle + ladder
    denom = (eps_vir[None, None, None, :] + eps_vir[None, :, None, None]
             - eps_occ[:, None, None, None] - eps_occ[None, None, :, None])
    keep = pair_mask.astype(jnp.float32)[:, None, :, None]
    new_amps = (-total / denom * keep).astype(jnp.bfloat16)
    pair_energy = jnp.sum(integrals.astype(jnp.float32) * new_amps.astype(jnp.float32), axis=(1, 3)) / V
    return new_amps, pair_energy
```

```python
import functools

import jax
import jax.numpy as jnp
from jax import lax
from jax.experimental import pallas as pl
from jax.experimental.pallas import tpu as pltpu
from jax.sharding import PartitionSpec as P

F32, BF16 = jnp.float32, jnp.bfloat16
MESH = pl.DeviceIdType.MESH
TILE = 256
LANES = 128
K_PARTS = 2


def iota(shape, axis):
    return lax.broadcasted_iota(jnp.int32, shape, axis)


def dot(left, right):
    return jnp.dot(left, right, preferred_element_type=F32)


def kernel(
    n_occ, n_vir, nb, n_o,
    a_hbm, g_hbm, w_ref, eo_ref, ev_ref, mask_ref,
    new_hbm, en_ref,
    amps, panel, direct, wblk, acc, rden, newv, eall,
    load_sem, z_send, z_recv, x_send, x_recv, c_send, c_recv, e_send, e_recv, out_sem,
):
    ri, rows, n_v = g_hbm.shape
    n_x = n_occ // 2
    tiles = rows // TILE
    k_per = n_o // K_PARTS
    o_bits = n_o.bit_length() - 1
    chunks = [(i, h) for i in range(ri) for h in range(K_PARTS)]

    z = lax.axis_index("vir")
    m = lax.axis_index("occ")
    sib = m + 1 - 2 * lax.rem(m, 2)
    x_right = lax.rem(m + 2, n_occ)
    x_left = lax.rem(m + n_occ - 2, n_occ)

    def amps_block(origin):
        return amps.at[pl.ds(origin * ri, ri)]

    load_g = [
        pltpu.make_async_copy(g_hbm.at[i], direct.at[i], load_sem.at[i]) for i in range(ri)
    ]
    load_a = pltpu.make_async_copy(a_hbm, amps_block(m), load_sem.at[ri])
    for copy in load_g:
        copy.start()
    load_a.start()

    barrier = pltpu.get_barrier_semaphore()
    for d in range(1, n_vir):
        pl.semaphore_signal(
            barrier, inc=1, device_id={"vir": lax.rem(z + d, n_vir)}, device_id_type=MESH
        )
    for peer in (sib, x_right, x_left):
        pl.semaphore_signal(barrier, inc=1, device_id={"occ": peer}, device_id_type=MESH)

    c_sub = max(TILE // n_o, 16)
    part = c_sub * n_o
    sub_bits = c_sub.bit_length() - 1
    to_row = iota((part, part), 0)
    source = ((to_row & (c_sub - 1)) << o_bits) + (to_row >> sub_bits)
    shuffle = jnp.where(iota((part, part), 1) == source, 1.0, 0.0).astype(BF16)

    def permute(i):
        for s in range(nb // c_sub):
            block = dot(shuffle, direct[i, pl.ds(s * part, part), :]).astype(BF16)
            first = pl.multiple_of(z * nb + s * c_sub, c_sub)
            panel[i, :, pl.ds(first, c_sub), :] = block.reshape(n_o, c_sub, n_v)

    def z_copy(way, origin, q):
        i, h = chunks[q]
        first = pl.multiple_of(origin * nb, nb)
        block = panel.at[i, pl.ds(h * k_per, k_per), pl.ds(first, nb), :]
        target = jnp.clip(z + (1 if way == 0 else -1), 0, n_vir - 1)
        return pltpu.make_async_remote_copy(
            src_ref=block,
            dst_ref=block,
            send_sem=z_send.at[way, origin, q],
            recv_sem=z_recv.at[way, origin, q],
            device_id={"vir": target},
            device_id_type=MESH,
        )

    def has_next(way):
        return z < n_vir - 1 if way == 0 else z > 0

    def origin_of(way, step):
        return z - step if way == 0 else z + step

    def exists(way, step):
        return z - step >= 0 if way == 0 else z + step < n_vir

    def z_start(way, origin, q):
        z_copy(way, origin, q).start()

    def x_copy(step, source=None):
        origin = lax.rem(m + n_occ - 2 * step, n_occ)
        return pltpu.make_async_remote_copy(
            src_ref=amps_block(origin) if source is None else source,
            dst_ref=amps_block(origin),
            send_sem=x_send.at[step],
            recv_sem=x_recv.at[step],
            device_id={"occ": x_right},
            device_id_type=MESH,
        )

    def c_copy(step, source=None):
        origin = lax.rem(m + n_occ - 2 * step, n_occ)
        return pltpu.make_async_remote_copy(
            src_ref=amps_block(origin) if source is None else source,
            dst_ref=amps_block(origin),
            send_sem=c_send.at[step],
            recv_sem=c_recv.at[step],
            device_id={"occ": sib},
            device_id_type=MESH,
        )

    def e_copy(d, i):
        return pltpu.make_async_remote_copy(
            src_ref=eall.at[z, i],
            dst_ref=eall.at[z, i],
            send_sem=e_send.at[d, i],
            recv_sem=e_recv.at[d, i],
            device_id={"vir": lax.rem(z + d, n_vir)},
            device_id_type=MESH,
        )

    def e_arrival(d, i):
        origin = lax.rem(z + n_vir - d, n_vir)
        return pltpu.make_async_remote_copy(
            src_ref=eall.at[origin, i],
            dst_ref=eall.at[origin, i],
            send_sem=e_send.at[d, i],
            recv_sem=e_recv.at[d, i],
            device_id={"vir": origin},
            device_id_type=MESH,
        )

    load_g[0].wait()
    permute(0)
    pl.semaphore_wait(barrier, n_vir + 2)
    for i in range(ri):
        if i:
            load_g[i].wait()
            permute(i)
        for q, (qi, _) in enumerate(chunks):
            if qi == i:
                for way in (0, 1):
                    pl.when(has_next(way))(functools.partial(z_start, way, z, q))
        if i == 0:
            load_a.wait()
            if n_x > 1:
                x_copy(0).start()
            c_copy(0).start()

    row = iota((TILE, 1), 0)
    row_j = row & (n_o - 1)
    eps_j = jnp.zeros((TILE, 1), F32)
    keep = [jnp.zeros((TILE, 1), F32) for _ in range(ri)]
    for j in range(n_o):
        eps_j = jnp.where(row_j == j, eo_ref[j], eps_j)
        for i in range(ri):
            keep[i] = jnp.where(row_j == j, mask_ref[i, j].astype(F32), keep[i])
    ev = ev_ref[...]

    def factors(t, carry):
        own = iota((TILE, n_v), 1) == z * nb + ((t * TILE + iota((TILE, n_v), 0)) >> o_bits)
        eps_b = jnp.sum(jnp.where(own, ev, 0.0), axis=1, keepdims=True)
        for i in range(ri):
            denom = ((ev + eps_b) - eo_ref[m * ri + i]) - eps_j
            rden[i, pl.ds(pl.multiple_of(t * TILE, TILE), TILE), :] = -keep[i] / denom
        return carry

    lax.fori_loop(0, tiles, factors, 0)

    up = jnp.where((iota((TILE, n_o), 0) & (n_o - 1)) == iota((TILE, n_o), 1), 1.0, 0.0)
    across = jnp.where((iota((n_o, TILE), 1) & (n_o - 1)) == iota((n_o, TILE), 0), 1.0, 0.0)
    same_b = (iota((TILE, TILE), 0) >> o_bits) == (iota((TILE, TILE), 1) >> o_bits)
    for i in range(ri):
        w_i = w_ref[i].astype(F32)

        def spread(k, carry, i=i, w_i=w_i):
            w_k = jnp.sum(jnp.where(iota(w_i.shape, 1) == k, w_i, 0.0), axis=1)
            full = dot(up, dot(w_k, across))
            wblk[i, k] = jnp.where(same_b, full, 0.0).astype(BF16)
            return carry

        lax.fori_loop(0, n_o, spread, 0)

    def forward(step, q):
        for way in (0, 1):

            def take(way=way):
                z_copy(way, origin_of(way, step), q).wait_recv()
                pl.when(has_next(way))(
                    functools.partial(z_start, way, origin_of(way, step), q)
                )

            pl.when(exists(way, step))(take)

    def rows_of(t):
        return pl.ds(pl.multiple_of(t * TILE, TILE), TILE)

    def ladder(i):
        def body(t, carry):
            value = direct[i, rows_of(t), :].astype(F32)

            def add(k8, value):
                for kk in range(8):
                    k = k8 * 8 + kk
                    value = value + dot(wblk[i, k], amps[k, rows_of(t), :])
                return value

            acc[i, rows_of(t), :] = lax.fori_loop(0, n_o // 8, add, value)
            return carry

        lax.fori_loop(0, tiles, body, 0)

    def cycle(q, last):
        i, h = chunks[q]

        def body(t, carry):
            value = acc[i, rows_of(t), :]

            def add(k4, value):
                for kk in range(4):
                    k = h * k_per + k4 * 4 + kk
                    value = value + dot(amps[k, rows_of(t), :], panel[i, k])
                return value

            value = lax.fori_loop(0, k_per // 4, add, value)
            if not last:
                acc[i, rows_of(t), :] = value
                return carry
            new = (value * rden[i, rows_of(t), :]).astype(BF16)
            newv[i, rows_of(t), :] = new
            prod = direct[i, rows_of(t), :].astype(F32) * new.astype(F32)
            return carry + jnp.sum(prod.reshape(TILE // n_o, n_o, n_v), axis=0)

        if not last:
            lax.fori_loop(0, tiles, body, 0)
            return
        energy = lax.fori_loop(0, tiles, body, jnp.zeros((n_o, n_v), F32))
        out = pltpu.make_async_copy(newv.at[i], new_hbm.at[i], out_sem.at[i])
        out.start()
        folded = energy[:, :LANES]
        for s in range(1, n_v // LANES):
            folded = folded + energy[:, s * LANES : (s + 1) * LANES]
        eall[z, i] = folded
        for d in range(1, n_vir):
            e_copy(d, i).start()

    def amps_step(step):
        if step:
            x_copy(step - 1).wait_recv()
            if step < n_x - 1:
                x_copy(step).start()
            c_copy(step).start()

    work = [functools.partial(amps_step, s) for s in range(1, n_x)]

    def all_amps():
        for s in range(n_x):
            c_copy(s).wait_recv()

    tail_work = [all_amps] + [functools.partial(ladder, i) for i in range(ri)]
    slots = []
    for step in range(1, n_vir - 1):
        for q in range(len(chunks)):
            slots.append((step, q))
    for index, (step, q) in enumerate(slots):
        forward(step, q)
        if work:
            work.pop(0)()
        elif index >= len(chunks) and tail_work:
            tail_work.pop(0)()
    for piece in work + tail_work:
        piece()
    for q, (i, h) in enumerate(chunks):
        forward(n_vir - 1, q)
        cycle(q, h == K_PARTS - 1)

    for i in range(ri):
        for d in range(1, n_vir):
            e_arrival(d, i).wait_recv()
        total = eall[0, i]
        for s in range(1, n_vir):
            total = total + eall[s, i]
        column = jnp.sum(total, axis=1, keepdims=True) / n_v
        spot = iota((n_o, LANES), 0) == iota((n_o, LANES), 1)
        line = jnp.sum(jnp.where(spot, column, 0.0), axis=0, keepdims=True)
        en_ref[pl.ds(i, 1), :] = line[:, :n_o]

    for way in (0, 1):
        for step in range(n_vir):
            for q in range(len(chunks)):

                def sent(way=way, step=step, q=q):
                    z_copy(way, origin_of(way, step), q).wait_send()

                pl.when(jnp.logical_and(has_next(way), exists(way, step)))(sent)
    for s in range(n_x):
        if s < n_x - 1:
            x_copy(s).wait_send()
        c_copy(s).wait_send()
    for i in range(ri):
        for d in range(1, n_vir):
            e_copy(d, i).wait_send()
        pltpu.make_async_copy(newv.at[i], new_hbm.at[i], out_sem.at[i]).wait()


def per_device(n_occ, n_vir, amps, integrals, ladder_ints, eps_occ, eps_vir, pair_mask):
    ri, nb, n_o, n_v = amps.shape
    rows = nb * n_o
    n_chunks = ri * K_PARTS
    n_x = n_occ // 2
    flops = 2 * 2 * ri * rows * n_v * n_o * n_v
    dma = pltpu.SemaphoreType.DMA
    new, energy = pl.pallas_call(
        functools.partial(kernel, n_occ, n_vir, nb, n_o),
        out_shape=(
            jax.ShapeDtypeStruct((ri, rows, n_v), BF16),
            jax.ShapeDtypeStruct((ri, n_o), F32),
        ),
        in_specs=[
            pl.BlockSpec(memory_space=pl.ANY),
            pl.BlockSpec(memory_space=pl.ANY),
            pl.BlockSpec(memory_space=pltpu.VMEM),
            pl.BlockSpec(memory_space=pltpu.SMEM),
            pl.BlockSpec(memory_space=pltpu.VMEM),
            pl.BlockSpec(memory_space=pltpu.SMEM),
        ],
        out_specs=(
            pl.BlockSpec(memory_space=pl.ANY),
            pl.BlockSpec(memory_space=pltpu.VMEM),
        ),
        scratch_shapes=[
            pltpu.VMEM((n_o, rows, n_v), BF16),
            pltpu.VMEM((ri, n_o, n_v, n_v), BF16),
            pltpu.VMEM((ri, rows, n_v), BF16),
            pltpu.VMEM((ri, n_o, TILE, TILE), BF16),
            pltpu.VMEM((ri, rows, n_v), F32),
            pltpu.VMEM((ri, rows, n_v), F32),
            pltpu.VMEM((ri, rows, n_v), BF16),
            pltpu.VMEM((n_vir, ri, n_o, LANES), F32),
            dma((ri + 1,)),
            dma((2, n_vir, n_chunks)),
            dma((2, n_vir, n_chunks)),
            dma((n_x,)),
            dma((n_x,)),
            dma((n_x,)),
            dma((n_x,)),
            dma((n_vir, ri)),
            dma((n_vir, ri)),
            dma((ri,)),
        ],
        compiler_params=pltpu.CompilerParams(
            collective_id=0, has_side_effects=True, vmem_limit_bytes=56 * 2**20
        ),
        cost_estimate=pl.CostEstimate(
            flops=flops, bytes_accessed=3 * ri * rows * n_v * 2, transcendentals=0
        ),
    )(
        amps.reshape(ri, rows, n_v),
        integrals.reshape(ri, rows, n_v),
        ladder_ints,
        eps_occ,
        eps_vir.reshape(1, n_v),
        pair_mask,
    )
    return new.reshape(ri, nb, n_o, n_v), energy


def solution(mesh):
    in_specs = (
        P(("groups", "occ"), "vir", None, None),
        P(("groups", "occ"), "vir", None, None),
        P(("groups", "occ"), None, None, None),
        P("groups"),
        P("groups"),
        P(("groups", "occ"), None),
    )
    out_specs = (P(("groups", "occ"), "vir", None, None), P(("groups", "occ"), None))
    body = functools.partial(per_device, mesh.shape["occ"], mesh.shape["vir"])
    return jax.shard_map(
        body, mesh=mesh, in_specs=in_specs, out_specs=out_specs, check_vma=False
    )
```

```python
import functools

import jax
import jax.numpy as jnp
from jax import lax
from jax.experimental import pallas as pl
from jax.experimental.pallas import tpu as pltpu
from jax.sharding import PartitionSpec as P

F32, BF16 = jnp.float32, jnp.bfloat16
MESH = pl.DeviceIdType.MESH
TILE = 256
LANES = 128
K_PARTS = 2


def iota(shape, axis):
    return lax.broadcasted_iota(jnp.int32, shape, axis)


def dot(left, right):
    return jnp.dot(left, right, preferred_element_type=F32)


def kernel(
    n_occ, n_vir, nb, n_o, lend,
    a_hbm, g_hbm, w_ref, eo_ref, ev_ref, mask_ref,
    new_hbm, en_ref,
    amps, panel, direct, wblk, acc, rden, newv, eall,
    amps2, direct2, rden2, new2,
    load_sem, z_send, z_recv, x_send, x_recv, c_send, c_recv, e_send, e_recv, out_sem,
    t_send, t_recv, tx_send, tx_recv, tc_send, tc_recv, r_send, r_recv,
):
    ri, rows, n_v = g_hbm.shape
    n_x = n_occ // 2
    tiles = rows // TILE
    k_per = n_o // K_PARTS
    o_bits = n_o.bit_length() - 1
    chunks = [(i, h) for i in range(ri) for h in range(K_PARTS)]

    z = lax.axis_index("vir")
    m = lax.axis_index("occ")
    sib = m + 1 - 2 * lax.rem(m, 2)
    x_right = lax.rem(m + 2, n_occ)
    x_left = lax.rem(m + n_occ - 2, n_occ)

    def amps_block(origin):
        return amps.at[pl.ds(origin * ri, ri)]

    load_g = [
        pltpu.make_async_copy(g_hbm.at[i], direct.at[i], load_sem.at[i]) for i in range(ri)
    ]
    load_a = pltpu.make_async_copy(a_hbm, amps_block(m), load_sem.at[ri])
    for copy in load_g:
        copy.start()
    load_a.start()

    barrier = pltpu.get_barrier_semaphore()
    for d in range(1, n_vir):
        pl.semaphore_signal(
            barrier, inc=1, device_id={"vir": lax.rem(z + d, n_vir)}, device_id_type=MESH
        )
    for peer in (sib, x_right, x_left):
        pl.semaphore_signal(barrier, inc=1, device_id={"occ": peer}, device_id_type=MESH)

    c_sub = max(TILE // n_o, 16)
    part = c_sub * n_o
    sub_bits = c_sub.bit_length() - 1
    to_row = iota((part, part), 0)
    source = ((to_row & (c_sub - 1)) << o_bits) + (to_row >> sub_bits)
    shuffle = jnp.where(iota((part, part), 1) == source, 1.0, 0.0).astype(BF16)

    def permute(i):
        for s in range(nb // c_sub):
            block = dot(shuffle, direct[i, pl.ds(s * part, part), :]).astype(BF16)
            first = pl.multiple_of(z * nb + s * c_sub, c_sub)
            panel[i, :, pl.ds(first, c_sub), :] = block.reshape(n_o, c_sub, n_v)

    def z_copy(way, origin, q):
        i, h = chunks[q]
        first = pl.multiple_of(origin * nb, nb)
        block = panel.at[i, pl.ds(h * k_per, k_per), pl.ds(first, nb), :]
        target = jnp.clip(z + (1 if way == 0 else -1), 0, n_vir - 1)
        return pltpu.make_async_remote_copy(
            src_ref=block,
            dst_ref=block,
            send_sem=z_send.at[way, origin, q],
            recv_sem=z_recv.at[way, origin, q],
            device_id={"vir": target},
            device_id_type=MESH,
        )

    last = ri - 1
    is_end = jnp.logical_or(z == 0, z == n_vir - 1)
    is_helper = jnp.logical_or(z == 1, z == n_vir - 2)
    low_half = z < n_vir // 2
    z_in = jnp.where(low_half, z + 1, z - 1)
    z_out = jnp.clip(jnp.where(low_half, z - 1, z + 1), 0, n_vir - 1)

    def lent(q):
        return lend and chunks[q][0] == last

    def has_next(way, q):
        margin = 1 if lent(q) else 0
        return z < n_vir - 1 - margin if way == 0 else z > margin

    def origin_of(way, step):
        return z - step if way == 0 else z + step

    def exists(way, step, q):
        there = z - step >= 0 if way == 0 else z + step < n_vir
        if lent(q) and step:
            there = jnp.logical_and(there, jnp.logical_not(is_end))
        return there

    def block2(origin, t):
        return amps2.at[pl.ds(origin * ri, ri), pl.ds(t * TILE, TILE), :]

    def t_copy(t):
        return pltpu.make_async_remote_copy(
            src_ref=amps.at[pl.ds(m * ri, ri), pl.ds(t * TILE, TILE), :],
            dst_ref=block2(m, t),
            send_sem=t_send.at[t],
            recv_sem=t_recv.at[t],
            device_id={"vir": z_in},
            device_id_type=MESH,
        )

    def tx_copy(step, t):
        block = block2(lax.rem(m + n_occ - 2 * step, n_occ), t)
        return pltpu.make_async_remote_copy(
            src_ref=block,
            dst_ref=block,
            send_sem=tx_send.at[step, t],
            recv_sem=tx_recv.at[step, t],
            device_id={"occ": x_right},
            device_id_type=MESH,
        )

    def tc_copy(step, t):
        block = block2(lax.rem(m + n_occ - 2 * step, n_occ), t)
        return pltpu.make_async_remote_copy(
            src_ref=block,
            dst_ref=block,
            send_sem=tc_send.at[step, t],
            recv_sem=tc_recv.at[step, t],
            device_id={"occ": sib},
            device_id_type=MESH,
        )

    def r_copy(t):
        return pltpu.make_async_remote_copy(
            src_ref=new2.at[pl.ds(t * TILE, TILE), :],
            dst_ref=newv.at[last, pl.ds(t * TILE, TILE), :],
            send_sem=r_send.at[t],
            recv_sem=r_recv.at[t],
            device_id={"vir": z_out},
            device_id_type=MESH,
        )

    def lend_amps():
        for t in range(tiles):
            t_copy(t).start()

    def helper_take():
        for t in range(tiles):
            t_copy(t).wait_recv()
            if n_x > 1:
                tx_copy(0, t).start()
            tc_copy(0, t).start()

    def helper_x():
        for step in range(1, n_x):
            for t in range(tiles):
                tx_copy(step - 1, t).wait_recv()
                if step < n_x - 1:
                    tx_copy(step, t).start()
                tc_copy(step, t).start()

    def z_start(way, origin, q):
        z_copy(way, origin, q).start()

    def x_copy(step, source=None):
        origin = lax.rem(m + n_occ - 2 * step, n_occ)
        return pltpu.make_async_remote_copy(
            src_ref=amps_block(origin) if source is None else source,
            dst_ref=amps_block(origin),
            send_sem=x_send.at[step],
            recv_sem=x_recv.at[step],
            device_id={"occ": x_right},
            device_id_type=MESH,
        )

    def c_copy(step, source=None):
        origin = lax.rem(m + n_occ - 2 * step, n_occ)
        return pltpu.make_async_remote_copy(
            src_ref=amps_block(origin) if source is None else source,
            dst_ref=amps_block(origin),
            send_sem=c_send.at[step],
            recv_sem=c_recv.at[step],
            device_id={"occ": sib},
            device_id_type=MESH,
        )

    def e_copy(d, i):
        return pltpu.make_async_remote_copy(
            src_ref=eall.at[z, i],
            dst_ref=eall.at[z, i],
            send_sem=e_send.at[d, i],
            recv_sem=e_recv.at[d, i],
            device_id={"vir": lax.rem(z + d, n_vir)},
            device_id_type=MESH,
        )

    def e_arrival(d, i):
        origin = lax.rem(z + n_vir - d, n_vir)
        return pltpu.make_async_remote_copy(
            src_ref=eall.at[origin, i],
            dst_ref=eall.at[origin, i],
            send_sem=e_send.at[d, i],
            recv_sem=e_recv.at[d, i],
            device_id={"vir": origin},
            device_id_type=MESH,
        )

    load_g[0].wait()
    permute(0)
    pl.semaphore_wait(barrier, n_vir + 2)
    for i in range(ri):
        if i:
            load_g[i].wait()
            permute(i)
        for q, (qi, _) in enumerate(chunks):
            if qi == i:
                for way in (0, 1):
                    pl.when(has_next(way, q))(functools.partial(z_start, way, z, q))
        if i == 0:
            load_a.wait()
            if n_x > 1:
                x_copy(0).start()
            c_copy(0).start()
            if lend:
                pl.when(is_end)(lend_amps)

    row = iota((TILE, 1), 0)
    row_j = row & (n_o - 1)
    eps_j = jnp.zeros((TILE, 1), F32)
    keep = [jnp.zeros((TILE, 1), F32) for _ in range(ri)]
    for j in range(n_o):
        eps_j = jnp.where(row_j == j, eo_ref[j], eps_j)
        for i in range(ri):
            keep[i] = jnp.where(row_j == j, mask_ref[i, j].astype(F32), keep[i])
    ev = ev_ref[...]

    def factors(t, carry):
        own = iota((TILE, n_v), 1) == z * nb + ((t * TILE + iota((TILE, n_v), 0)) >> o_bits)
        eps_b = jnp.sum(jnp.where(own, ev, 0.0), axis=1, keepdims=True)
        for i in range(ri):
            denom = ((ev + eps_b) - eo_ref[m * ri + i]) - eps_j
            rden[i, pl.ds(pl.multiple_of(t * TILE, TILE), TILE), :] = -keep[i] / denom
        return carry

    lax.fori_loop(0, tiles, factors, 0)

    def factors2(t, carry):
        own = iota((TILE, n_v), 1) == z_out * nb + (
            (t * TILE + iota((TILE, n_v), 0)) >> o_bits
        )
        eps_b = jnp.sum(jnp.where(own, ev, 0.0), axis=1, keepdims=True)
        denom = ((ev + eps_b) - eo_ref[m * ri + last]) - eps_j
        rden2[pl.ds(pl.multiple_of(t * TILE, TILE), TILE), :] = -keep[last] / denom
        return carry

    if lend:
        lax.fori_loop(0, tiles, factors2, 0)

    up = jnp.where((iota((TILE, n_o), 0) & (n_o - 1)) == iota((TILE, n_o), 1), 1.0, 0.0)
    across = jnp.where((iota((n_o, TILE), 1) & (n_o - 1)) == iota((n_o, TILE), 0), 1.0, 0.0)
    same_b = (iota((TILE, TILE), 0) >> o_bits) == (iota((TILE, TILE), 1) >> o_bits)
    for i in range(ri):
        w_i = w_ref[i].astype(F32)

        def spread(k, carry, i=i, w_i=w_i):
            w_k = jnp.sum(jnp.where(iota(w_i.shape, 1) == k, w_i, 0.0), axis=1)
            full = dot(up, dot(w_k, across))
            wblk[i, k] = jnp.where(same_b, full, 0.0).astype(BF16)
            return carry

        lax.fori_loop(0, n_o, spread, 0)

    def forward(step, q):
        for way in (0, 1):

            def take(way=way):
                z_copy(way, origin_of(way, step), q).wait_recv()
                pl.when(has_next(way, q))(
                    functools.partial(z_start, way, origin_of(way, step), q)
                )

            pl.when(exists(way, step, q))(take)

    def rows_of(t):
        return pl.ds(pl.multiple_of(t * TILE, TILE), TILE)

    def ladder(i):
        def body(t, carry):
            value = direct[i, rows_of(t), :].astype(F32)

            def add(k8, value):
                for kk in range(8):
                    k = k8 * 8 + kk
                    value = value + dot(wblk[i, k], amps[k, rows_of(t), :])
                return value

            acc[i, rows_of(t), :] = lax.fori_loop(0, n_o // 8, add, value)
            return carry

        lax.fori_loop(0, tiles, body, 0)

    def cycle(q, last):
        i, h = chunks[q]

        def body(t, carry):
            value = acc[i, rows_of(t), :]

            def add(k4, value):
                for kk in range(4):
                    k = h * k_per + k4 * 4 + kk
                    value = value + dot(amps[k, rows_of(t), :], panel[i, k])
                return value

            value = lax.fori_loop(0, k_per // 4, add, value)
            if not last:
                acc[i, rows_of(t), :] = value
                return carry
            new = (value * rden[i, rows_of(t), :]).astype(BF16)
            newv[i, rows_of(t), :] = new
            prod = direct[i, rows_of(t), :].astype(F32) * new.astype(F32)
            return carry + jnp.sum(prod.reshape(TILE // n_o, n_o, n_v), axis=0)

        if not last:
            lax.fori_loop(0, tiles, body, 0)
            return
        finish(i, lax.fori_loop(0, tiles, body, jnp.zeros((n_o, n_v), F32)))

    def finish(i, energy):
        out = pltpu.make_async_copy(newv.at[i], new_hbm.at[i], out_sem.at[i])
        out.start()
        folded = energy[:, :LANES]
        for s in range(1, n_v // LANES):
            folded = folded + energy[:, s * LANES : (s + 1) * LANES]
        eall[z, i] = folded
        for d in range(1, n_vir):
            e_copy(d, i).start()

    def helper_rows():
        from_row = iota((part, part), 1)
        place = ((from_row & (c_sub - 1)) << o_bits) + (from_row >> sub_bits)
        back = jnp.where(iota((part, part), 0) == place, 1.0, 0.0).astype(BF16)
        for s in range(nb // c_sub):
            first = pl.multiple_of(z_out * nb + s * c_sub, c_sub)
            block = panel[last, :, pl.ds(first, c_sub), :].reshape(part, n_v)
            direct2[pl.ds(s * part, part), :] = dot(back, block).astype(BF16)
        for step in range(n_x):
            for t in range(tiles):
                tc_copy(step, t).wait_recv()
        for t in range(tiles):
            here = pl.ds(t * TILE, TILE)

            def add(k4, value, here=here):
                for kk in range(4):
                    k = k4 * 4 + kk
                    rows_k = amps2[k, here, :]
                    value = value + dot(wblk[last, k], rows_k)
                    value = value + dot(rows_k, panel[last, k])
                return value

            value = lax.fori_loop(0, n_o // 4, add, direct2[here, :].astype(F32))
            new2[here, :] = (value * rden2[here, :]).astype(BF16)
            r_copy(t).start()

    def end_rows():
        energy = jnp.zeros((n_o, n_v), F32)
        for t in range(tiles):
            here = pl.ds(t * TILE, TILE)
            r_copy(t).wait_recv()
            prod = direct[last, here, :].astype(F32) * newv[last, here, :].astype(F32)
            energy = energy + jnp.sum(prod.reshape(TILE // n_o, n_o, n_v), axis=0)
        finish(last, energy)

    def amps_step(step):
        if step:
            x_copy(step - 1).wait_recv()
            if step < n_x - 1:
                x_copy(step).start()
            c_copy(step).start()

    def all_amps():
        for s in range(n_x):
            c_copy(s).wait_recv()

    def helper_piece(piece):
        if lend:
            pl.when(is_helper)(piece)

    def ladder_piece(i):
        if lend and i == last:
            pl.when(jnp.logical_not(is_end))(functools.partial(ladder, i))
        else:
            ladder(i)

    work = [functools.partial(amps_step, s) for s in range(1, n_x)]
    work += [functools.partial(helper_piece, helper_x), all_amps]
    work += [functools.partial(ladder_piece, i) for i in range(ri)]
    for step in range(1, n_vir - 1):
        for q in range(len(chunks)):
            if step == 1 and lent(q) and not lent(q - 1):
                helper_piece(helper_take)
            forward(step, q)
            if (step > 1 or q == len(chunks) - 1) and work:
                work.pop(0)()
    for piece in work:
        piece()
    helper_piece(helper_rows)
    for q, (i, h) in enumerate(chunks):
        forward(n_vir - 1, q)
        piece = functools.partial(cycle, q, h == K_PARTS - 1)
        if lent(q):
            pl.when(jnp.logical_not(is_end))(piece)
        else:
            piece()
    if lend:
        pl.when(is_end)(end_rows)

    for i in range(ri):
        for d in range(1, n_vir):
            e_arrival(d, i).wait_recv()
        total = eall[0, i]
        for s in range(1, n_vir):
            total = total + eall[s, i]
        column = jnp.sum(total, axis=1, keepdims=True) / n_v
        spot = iota((n_o, LANES), 0) == iota((n_o, LANES), 1)
        line = jnp.sum(jnp.where(spot, column, 0.0), axis=0, keepdims=True)
        en_ref[pl.ds(i, 1), :] = line[:, :n_o]

    for way in (0, 1):
        for step in range(n_vir):
            for q in range(len(chunks)):

                def sent(way=way, step=step, q=q):
                    z_copy(way, origin_of(way, step), q).wait_send()

                pl.when(jnp.logical_and(has_next(way, q), exists(way, step, q)))(sent)
    for s in range(n_x):
        if s < n_x - 1:
            x_copy(s).wait_send()
        c_copy(s).wait_send()
    def helper_sent():
        for t in range(tiles):
            for s in range(n_x):
                if s < n_x - 1:
                    tx_copy(s, t).wait_send()
                tc_copy(s, t).wait_send()
            r_copy(t).wait_send()

    def end_sent():
        for t in range(tiles):
            t_copy(t).wait_send()

    if lend:
        pl.when(is_helper)(helper_sent)
        pl.when(is_end)(end_sent)
    for i in range(ri):
        for d in range(1, n_vir):
            e_copy(d, i).wait_send()
        pltpu.make_async_copy(newv.at[i], new_hbm.at[i], out_sem.at[i]).wait()


def per_device(n_occ, n_vir, amps, integrals, ladder_ints, eps_occ, eps_vir, pair_mask):
    ri, nb, n_o, n_v = amps.shape
    rows = nb * n_o
    n_chunks = ri * K_PARTS
    n_x = n_occ // 2
    flops = 2 * 2 * ri * rows * n_v * n_o * n_v
    dma = pltpu.SemaphoreType.DMA
    tiles = rows // TILE
    lend = n_vir >= 4 and n_o * rows * n_v * 2 <= 4 * 2**20
    extra = rows if lend else 16
    new, energy = pl.pallas_call(
        functools.partial(kernel, n_occ, n_vir, nb, n_o, lend),
        out_shape=(
            jax.ShapeDtypeStruct((ri, rows, n_v), BF16),
            jax.ShapeDtypeStruct((ri, n_o), F32),
        ),
        in_specs=[
            pl.BlockSpec(memory_space=pl.ANY),
            pl.BlockSpec(memory_space=pl.ANY),
            pl.BlockSpec(memory_space=pltpu.VMEM),
            pl.BlockSpec(memory_space=pltpu.SMEM),
            pl.BlockSpec(memory_space=pltpu.VMEM),
            pl.BlockSpec(memory_space=pltpu.SMEM),
        ],
        out_specs=(
            pl.BlockSpec(memory_space=pl.ANY),
            pl.BlockSpec(memory_space=pltpu.VMEM),
        ),
        scratch_shapes=[
            pltpu.VMEM((n_o, rows, n_v), BF16),
            pltpu.VMEM((ri, n_o, n_v, n_v), BF16),
            pltpu.VMEM((ri, rows, n_v), BF16),
            pltpu.VMEM((ri, n_o, TILE, TILE), BF16),
            pltpu.VMEM((ri, rows, n_v), F32),
            pltpu.VMEM((ri, rows, n_v), F32),
            pltpu.VMEM((ri, rows, n_v), BF16),
            pltpu.VMEM((n_vir, ri, n_o, LANES), F32),
            pltpu.VMEM((n_o, extra, n_v), BF16),
            pltpu.VMEM((extra, n_v), BF16),
            pltpu.VMEM((extra, n_v), F32),
            pltpu.VMEM((extra, n_v), BF16),
            dma((ri + 1,)),
            dma((2, n_vir, n_chunks)),
            dma((2, n_vir, n_chunks)),
            dma((n_x,)),
            dma((n_x,)),
            dma((n_x,)),
            dma((n_x,)),
            dma((n_vir, ri)),
            dma((n_vir, ri)),
            dma((ri,)),
            dma((tiles,)),
            dma((tiles,)),
            dma((n_x, tiles)),
            dma((n_x, tiles)),
            dma((n_x, tiles)),
            dma((n_x, tiles)),
            dma((tiles,)),
            dma((tiles,)),
        ],
        compiler_params=pltpu.CompilerParams(
            collective_id=0, has_side_effects=True, vmem_limit_bytes=56 * 2**20
        ),
        cost_estimate=pl.CostEstimate(
            flops=flops, bytes_accessed=3 * ri * rows * n_v * 2, transcendentals=0
        ),
    )(
        amps.reshape(ri, rows, n_v),
        integrals.reshape(ri, rows, n_v),
        ladder_ints,
        eps_occ,
        eps_vir.reshape(1, n_v),
        pair_mask,
    )
    return new.reshape(ri, nb, n_o, n_v), energy


def solution(mesh):
    in_specs = (
        P(("groups", "occ"), "vir", None, None),
        P(("groups", "occ"), "vir", None, None),
        P(("groups", "occ"), None, None, None),
        P("groups"),
        P("groups"),
        P(("groups", "occ"), None),
    )
    out_specs = (P(("groups", "occ"), "vir", None, None), P(("groups", "occ"), None))
    body = functools.partial(per_device, mesh.shape["occ"], mesh.shape["vir"])
    return jax.shard_map(
        body, mesh=mesh, in_specs=in_specs, out_specs=out_specs, check_vma=False
    )
```

```python
import functools

import jax
import jax.numpy as jnp
from jax import lax
from jax.experimental import pallas as pl
from jax.experimental.pallas import tpu as pltpu
from jax.sharding import PartitionSpec as P

F32, BF16 = jnp.float32, jnp.bfloat16
MESH = pl.DeviceIdType.MESH
TILE = 256
LANES = 128
K_PARTS = 2
STRIP = 128


def iota(shape, axis):
    return lax.broadcasted_iota(jnp.int32, shape, axis)


def dot(left, right):
    return jnp.dot(left, right, preferred_element_type=F32)


def kernel(
    n_occ, n_vir, nb, n_o, lend,
    a_hbm, g_hbm, w_ref, eo_ref, ev_ref, mask_ref,
    new_hbm, en_ref,
    amps, panel, direct, wblk, acc, rden, newv, eall,
    amps2, direct2, rden2, new2,
    load_sem, z_send, z_recv, x_send, x_recv, c_send, c_recv, e_send, e_recv, out_sem,
    t_send, t_recv, tx_send, tx_recv, tc_send, tc_recv, r_send, r_recv,
):
    ri, rows, n_v = g_hbm.shape
    n_x = n_occ // 2
    tiles = rows // TILE
    strips = rows // STRIP
    k_per = n_o // K_PARTS
    o_bits = n_o.bit_length() - 1
    chunks = [(i, h) for i in range(ri) for h in range(K_PARTS)]

    z = lax.axis_index("vir")
    m = lax.axis_index("occ")
    sib = m + 1 - 2 * lax.rem(m, 2)
    x_right = lax.rem(m + 2, n_occ)
    x_left = lax.rem(m + n_occ - 2, n_occ)

    def amps_block(origin):
        return amps.at[pl.ds(origin * ri, ri)]

    load_g = [
        pltpu.make_async_copy(g_hbm.at[i], direct.at[i], load_sem.at[i]) for i in range(ri)
    ]
    load_a = pltpu.make_async_copy(a_hbm, amps_block(m), load_sem.at[ri])
    for copy in load_g:
        copy.start()
    load_a.start()

    barrier = pltpu.get_barrier_semaphore()
    for d in range(1, n_vir):
        pl.semaphore_signal(
            barrier, inc=1, device_id={"vir": lax.rem(z + d, n_vir)}, device_id_type=MESH
        )
    for peer in (sib, x_right, x_left):
        pl.semaphore_signal(barrier, inc=1, device_id={"occ": peer}, device_id_type=MESH)

    c_sub = max(TILE // n_o, 16)
    part = c_sub * n_o
    sub_bits = c_sub.bit_length() - 1
    to_row = iota((part, part), 0)
    source = ((to_row & (c_sub - 1)) << o_bits) + (to_row >> sub_bits)
    shuffle = jnp.where(iota((part, part), 1) == source, 1.0, 0.0).astype(BF16)

    def permute(i):
        for s in range(nb // c_sub):
            block = dot(shuffle, direct[i, pl.ds(s * part, part), :]).astype(BF16)
            first = pl.multiple_of(z * nb + s * c_sub, c_sub)
            panel[i, :, pl.ds(first, c_sub), :] = block.reshape(n_o, c_sub, n_v)

    def z_copy(way, origin, q):
        i, h = chunks[q]
        first = pl.multiple_of(origin * nb, nb)
        block = panel.at[i, pl.ds(h * k_per, k_per), pl.ds(first, nb), :]
        target = jnp.clip(z + (1 if way == 0 else -1), 0, n_vir - 1)
        return pltpu.make_async_remote_copy(
            src_ref=block,
            dst_ref=block,
            send_sem=z_send.at[way, origin, q],
            recv_sem=z_recv.at[way, origin, q],
            device_id={"vir": target},
            device_id_type=MESH,
        )

    last = ri - 1
    is_end = jnp.logical_or(z == 0, z == n_vir - 1)
    is_helper = jnp.logical_or(z == 1, z == n_vir - 2)
    low_half = z < n_vir // 2
    z_in = jnp.where(low_half, z + 1, z - 1)
    z_out = jnp.clip(jnp.where(low_half, z - 1, z + 1), 0, n_vir - 1)

    def lent(q):
        return lend and chunks[q][0] == last

    def has_next(way, q):
        margin = 1 if lent(q) else 0
        return z < n_vir - 1 - margin if way == 0 else z > margin

    def origin_of(way, step):
        return z - step if way == 0 else z + step

    def exists(way, step, q):
        there = z - step >= 0 if way == 0 else z + step < n_vir
        if lent(q) and step:
            there = jnp.logical_and(there, jnp.logical_not(is_end))
        return there

    def block2(origin, t):
        return amps2.at[pl.ds(origin * ri, ri), pl.ds(t * STRIP, STRIP), :]

    def t_copy(t):
        return pltpu.make_async_remote_copy(
            src_ref=amps.at[pl.ds(m * ri, ri), pl.ds(t * STRIP, STRIP), :],
            dst_ref=block2(m, t),
            send_sem=t_send.at[t],
            recv_sem=t_recv.at[t],
            device_id={"vir": z_in},
            device_id_type=MESH,
        )

    def tx_copy(step, t):
        block = block2(lax.rem(m + n_occ - 2 * step, n_occ), t)
        return pltpu.make_async_remote_copy(
            src_ref=block,
            dst_ref=block,
            send_sem=tx_send.at[step, t],
            recv_sem=tx_recv.at[step, t],
            device_id={"occ": x_right},
            device_id_type=MESH,
        )

    def tc_copy(step, t):
        block = block2(lax.rem(m + n_occ - 2 * step, n_occ), t)
        return pltpu.make_async_remote_copy(
            src_ref=block,
            dst_ref=block,
            send_sem=tc_send.at[step, t],
            recv_sem=tc_recv.at[step, t],
            device_id={"occ": sib},
            device_id_type=MESH,
        )

    def r_copy(t):
        return pltpu.make_async_remote_copy(
            src_ref=new2.at[pl.ds(t * STRIP, STRIP), :],
            dst_ref=newv.at[last, pl.ds(t * STRIP, STRIP), :],
            send_sem=r_send.at[t],
            recv_sem=r_recv.at[t],
            device_id={"vir": z_out},
            device_id_type=MESH,
        )

    def lend_amps():
        for t in range(strips):
            t_copy(t).start()

    def helper_take(t):
        t_copy(t).wait_recv()
        if n_x > 1:
            tx_copy(0, t).start()
        tc_copy(0, t).start()

    def helper_x(t):
        for step in range(1, n_x):
            tx_copy(step - 1, t).wait_recv()
            if step < n_x - 1:
                tx_copy(step, t).start()
            tc_copy(step, t).start()

    def z_start(way, origin, q):
        z_copy(way, origin, q).start()

    def x_copy(step, source=None):
        origin = lax.rem(m + n_occ - 2 * step, n_occ)
        return pltpu.make_async_remote_copy(
            src_ref=amps_block(origin) if source is None else source,
            dst_ref=amps_block(origin),
            send_sem=x_send.at[step],
            recv_sem=x_recv.at[step],
            device_id={"occ": x_right},
            device_id_type=MESH,
        )

    def c_copy(step, source=None):
        origin = lax.rem(m + n_occ - 2 * step, n_occ)
        return pltpu.make_async_remote_copy(
            src_ref=amps_block(origin) if source is None else source,
            dst_ref=amps_block(origin),
            send_sem=c_send.at[step],
            recv_sem=c_recv.at[step],
            device_id={"occ": sib},
            device_id_type=MESH,
        )

    def e_copy(d, i):
        return pltpu.make_async_remote_copy(
            src_ref=eall.at[z, i],
            dst_ref=eall.at[z, i],
            send_sem=e_send.at[d, i],
            recv_sem=e_recv.at[d, i],
            device_id={"vir": lax.rem(z + d, n_vir)},
            device_id_type=MESH,
        )

    def e_arrival(d, i):
        origin = lax.rem(z + n_vir - d, n_vir)
        return pltpu.make_async_remote_copy(
            src_ref=eall.at[origin, i],
            dst_ref=eall.at[origin, i],
            send_sem=e_send.at[d, i],
            recv_sem=e_recv.at[d, i],
            device_id={"vir": origin},
            device_id_type=MESH,
        )

    load_g[0].wait()
    permute(0)
    pl.semaphore_wait(barrier, n_vir + 2)
    if lend:
        load_a.wait()
        pl.when(is_end)(lend_amps)
    for i in range(ri):
        if i:
            load_g[i].wait()
            permute(i)
        for q, (qi, _) in enumerate(chunks):
            if qi == i:
                for way in (0, 1):
                    pl.when(has_next(way, q))(functools.partial(z_start, way, z, q))
        if i == 0:
            if not lend:
                load_a.wait()
            if n_x > 1:
                x_copy(0).start()
            c_copy(0).start()

    row = iota((TILE, 1), 0)
    row_j = row & (n_o - 1)
    eps_j = jnp.zeros((TILE, 1), F32)
    keep = [jnp.zeros((TILE, 1), F32) for _ in range(ri)]
    for j in range(n_o):
        eps_j = jnp.where(row_j == j, eo_ref[j], eps_j)
        for i in range(ri):
            keep[i] = jnp.where(row_j == j, mask_ref[i, j].astype(F32), keep[i])
    ev = ev_ref[...]

    def factors(t, carry):
        own = iota((TILE, n_v), 1) == z * nb + ((t * TILE + iota((TILE, n_v), 0)) >> o_bits)
        eps_b = jnp.sum(jnp.where(own, ev, 0.0), axis=1, keepdims=True)
        for i in range(ri):
            denom = ((ev + eps_b) - eo_ref[m * ri + i]) - eps_j
            rden[i, pl.ds(pl.multiple_of(t * TILE, TILE), TILE), :] = -keep[i] / denom
        return carry

    lax.fori_loop(0, tiles, factors, 0)

    def factors2(t, carry):
        own = iota((TILE, n_v), 1) == z_out * nb + (
            (t * TILE + iota((TILE, n_v), 0)) >> o_bits
        )
        eps_b = jnp.sum(jnp.where(own, ev, 0.0), axis=1, keepdims=True)
        denom = ((ev + eps_b) - eo_ref[m * ri + last]) - eps_j
        rden2[pl.ds(pl.multiple_of(t * TILE, TILE), TILE), :] = -keep[last] / denom
        return carry

    if lend:
        lax.fori_loop(0, tiles, factors2, 0)

    up = jnp.where((iota((TILE, n_o), 0) & (n_o - 1)) == iota((TILE, n_o), 1), 1.0, 0.0)
    across = jnp.where((iota((n_o, TILE), 1) & (n_o - 1)) == iota((n_o, TILE), 0), 1.0, 0.0)
    same_b = (iota((TILE, TILE), 0) >> o_bits) == (iota((TILE, TILE), 1) >> o_bits)
    for i in range(ri):
        w_i = w_ref[i].astype(F32)

        def spread(k, carry, i=i, w_i=w_i):
            w_k = jnp.sum(jnp.where(iota(w_i.shape, 1) == k, w_i, 0.0), axis=1)
            full = dot(up, dot(w_k, across))
            wblk[i, k] = jnp.where(same_b, full, 0.0).astype(BF16)
            return carry

        lax.fori_loop(0, n_o, spread, 0)

    def forward(step, q, side=None):
        for way in (0, 1):
            inner = low_half if way == 1 else jnp.logical_not(low_half)
            now = exists(way, step, q)
            if side == "in":
                now = jnp.logical_and(now, jnp.logical_or(jnp.logical_not(is_helper), inner))
            if side == "out":
                outer = jnp.logical_and(is_helper, jnp.logical_not(inner))
                now = jnp.logical_and(now, outer)

            def take(way=way):
                z_copy(way, origin_of(way, step), q).wait_recv()
                pl.when(has_next(way, q))(
                    functools.partial(z_start, way, origin_of(way, step), q)
                )

            pl.when(now)(take)

    def rows_of(t):
        return pl.ds(pl.multiple_of(t * TILE, TILE), TILE)

    def ladder(i):
        def body(t, carry):
            value = direct[i, rows_of(t), :].astype(F32)

            def add(k8, value):
                for kk in range(8):
                    k = k8 * 8 + kk
                    value = value + dot(wblk[i, k], amps[k, rows_of(t), :])
                return value

            acc[i, rows_of(t), :] = lax.fori_loop(0, n_o // 8, add, value)
            return carry

        lax.fori_loop(0, tiles, body, 0)

    def cycle(q, last):
        i, h = chunks[q]

        def body(t, carry):
            value = acc[i, rows_of(t), :]

            def add(k4, value):
                for kk in range(4):
                    k = h * k_per + k4 * 4 + kk
                    value = value + dot(amps[k, rows_of(t), :], panel[i, k])
                return value

            value = lax.fori_loop(0, k_per // 4, add, value)
            if not last:
                acc[i, rows_of(t), :] = value
                return carry
            new = (value * rden[i, rows_of(t), :]).astype(BF16)
            newv[i, rows_of(t), :] = new
            prod = direct[i, rows_of(t), :].astype(F32) * new.astype(F32)
            return carry + jnp.sum(prod.reshape(TILE // n_o, n_o, n_v), axis=0)

        if not last:
            lax.fori_loop(0, tiles, body, 0)
            return
        finish(i, lax.fori_loop(0, tiles, body, jnp.zeros((n_o, n_v), F32)))

    def finish(i, energy):
        out = pltpu.make_async_copy(newv.at[i], new_hbm.at[i], out_sem.at[i])
        out.start()
        folded = energy[:, :LANES]
        for s in range(1, n_v // LANES):
            folded = folded + energy[:, s * LANES : (s + 1) * LANES]
        eall[z, i] = folded
        for d in range(1, n_vir):
            e_copy(d, i).start()

    def helper_rows():
        from_row = iota((part, part), 1)
        place = ((from_row & (c_sub - 1)) << o_bits) + (from_row >> sub_bits)
        back = jnp.where(iota((part, part), 0) == place, 1.0, 0.0).astype(BF16)
        for s in range(nb // c_sub):
            first = pl.multiple_of(z_out * nb + s * c_sub, c_sub)
            block = panel[last, :, pl.ds(first, c_sub), :].reshape(part, n_v)
            direct2[pl.ds(s * part, part), :] = dot(back, block).astype(BF16)

        for t in range(strips):
            ahead = t + 2
            if ahead < strips:
                helper_x(ahead)
            for step in range(n_x):
                tc_copy(step, t).wait_recv()
            here = pl.ds(t * STRIP, STRIP)

            def add(k4, value, here=here):
                for kk in range(4):
                    k = k4 * 4 + kk
                    rows_k = amps2[k, here, :]
                    value = value + dot(wblk[last, k, :STRIP, :STRIP], rows_k)
                    value = value + dot(rows_k, panel[last, k])
                return value

            value = lax.fori_loop(0, n_o // 4, add, direct2[here, :].astype(F32))
            new2[here, :] = (value * rden2[here, :]).astype(BF16)
            r_copy(t).start()

    def end_rows():
        energy = jnp.zeros((n_o, n_v), F32)
        for t in range(strips):
            here = pl.ds(t * STRIP, STRIP)
            r_copy(t).wait_recv()
            prod = direct[last, here, :].astype(F32) * newv[last, here, :].astype(F32)
            energy = energy + jnp.sum(prod.reshape(STRIP // n_o, n_o, n_v), axis=0)
        finish(last, energy)

    def amps_step(step):
        if step:
            x_copy(step - 1).wait_recv()
            if step < n_x - 1:
                x_copy(step).start()
            c_copy(step).start()

    def all_amps():
        for s in range(n_x):
            c_copy(s).wait_recv()

    def helper_piece(piece):
        if lend:
            pl.when(is_helper)(piece)

    def ladder_piece(i):
        if lend and i == last:
            pl.when(jnp.logical_not(is_end))(functools.partial(ladder, i))
        else:
            ladder(i)

    if lend:
        n_q = len(chunks)
        for q in range(max(n_q, strips)):
            if q < n_q:
                forward(1, q, "in")
            if q < strips:
                helper_piece(functools.partial(helper_take, q))
        for s in range(1, n_x):
            amps_step(s)
        for step in range(2, n_vir - 1):
            for q in range(n_q):
                if step == 2:
                    forward(1, q, "out")
                forward(step, q)
                if step > 2:
                    continue
                if q == 1:
                    all_amps()
                    ladder_piece(0)
                    helper_piece(functools.partial(helper_x, 0))
                if q == 2:
                    for i in range(1, ri):
                        ladder_piece(i)
                    helper_piece(functools.partial(helper_x, 1))
    else:
        work = [functools.partial(amps_step, s) for s in range(1, n_x)] + [all_amps]
        work += [functools.partial(ladder_piece, i) for i in range(ri)]
        for step in range(1, n_vir - 1):
            for q in range(len(chunks)):
                forward(step, q)
                if (step > 1 or q == len(chunks) - 1) and work:
                    work.pop(0)()
        for piece in work:
            piece()
    helper_piece(helper_rows)
    for q, (i, h) in enumerate(chunks):
        forward(n_vir - 1, q)
        piece = functools.partial(cycle, q, h == K_PARTS - 1)
        if lent(q):
            pl.when(jnp.logical_not(is_end))(piece)
        else:
            piece()
    if lend:
        pl.when(is_end)(end_rows)

    for i in range(ri):
        for d in range(1, n_vir):
            e_arrival(d, i).wait_recv()
        total = eall[0, i]
        for s in range(1, n_vir):
            total = total + eall[s, i]
        column = jnp.sum(total, axis=1, keepdims=True) / n_v
        spot = iota((n_o, LANES), 0) == iota((n_o, LANES), 1)
        line = jnp.sum(jnp.where(spot, column, 0.0), axis=0, keepdims=True)
        en_ref[pl.ds(i, 1), :] = line[:, :n_o]

    for way in (0, 1):
        for step in range(n_vir):
            for q in range(len(chunks)):

                def sent(way=way, step=step, q=q):
                    z_copy(way, origin_of(way, step), q).wait_send()

                pl.when(jnp.logical_and(has_next(way, q), exists(way, step, q)))(sent)
    for s in range(n_x):
        if s < n_x - 1:
            x_copy(s).wait_send()
        c_copy(s).wait_send()
    def helper_sent():
        for t in range(strips):
            for s in range(n_x):
                if s < n_x - 1:
                    tx_copy(s, t).wait_send()
                tc_copy(s, t).wait_send()
            r_copy(t).wait_send()

    def end_sent():
        for t in range(strips):
            t_copy(t).wait_send()

    if lend:
        pl.when(is_helper)(helper_sent)
        pl.when(is_end)(end_sent)
    for i in range(ri):
        for d in range(1, n_vir):
            e_copy(d, i).wait_send()
        pltpu.make_async_copy(newv.at[i], new_hbm.at[i], out_sem.at[i]).wait()


def per_device(n_occ, n_vir, amps, integrals, ladder_ints, eps_occ, eps_vir, pair_mask):
    ri, nb, n_o, n_v = amps.shape
    rows = nb * n_o
    n_chunks = ri * K_PARTS
    n_x = n_occ // 2
    flops = 2 * 2 * ri * rows * n_v * n_o * n_v
    dma = pltpu.SemaphoreType.DMA
    strips = rows // STRIP
    lend = n_vir >= 4 and n_o * rows * n_v * 2 <= 4 * 2**20
    extra = rows if lend else 16
    new, energy = pl.pallas_call(
        functools.partial(kernel, n_occ, n_vir, nb, n_o, lend),
        out_shape=(
            pltpu.VMEM((ri, rows, n_v), BF16),
            pltpu.VMEM((ri, n_o), F32),
        ),
        in_specs=[
            pl.BlockSpec(memory_space=pl.ANY),
            pl.BlockSpec(memory_space=pl.ANY),
            pl.BlockSpec(memory_space=pltpu.VMEM),
            pl.BlockSpec(memory_space=pltpu.SMEM),
            pl.BlockSpec(memory_space=pltpu.VMEM),
            pl.BlockSpec(memory_space=pltpu.SMEM),
        ],
        out_specs=(
            pl.BlockSpec(memory_space=pltpu.VMEM),
            pl.BlockSpec(memory_space=pltpu.VMEM),
        ),
        scratch_shapes=[
            pltpu.VMEM((n_o, rows, n_v), BF16),
            pltpu.VMEM((ri, n_o, n_v, n_v), BF16),
            pltpu.VMEM((ri, rows, n_v), BF16),
            pltpu.VMEM((ri, n_o, TILE, TILE), BF16),
            pltpu.VMEM((ri, rows, n_v), F32),
            pltpu.VMEM((ri, rows, n_v), F32),
            pltpu.VMEM((ri, rows, n_v), BF16),
            pltpu.VMEM((n_vir, ri, n_o, LANES), F32),
            pltpu.VMEM((n_o, extra, n_v), BF16),
            pltpu.VMEM((extra, n_v), BF16),
            pltpu.VMEM((extra, n_v), F32),
            pltpu.VMEM((extra, n_v), BF16),
            dma((ri + 1,)),
            dma((2, n_vir, n_chunks)),
            dma((2, n_vir, n_chunks)),
            dma((n_x,)),
            dma((n_x,)),
            dma((n_x,)),
            dma((n_x,)),
            dma((n_vir, ri)),
            dma((n_vir, ri)),
            dma((ri,)),
            dma((strips,)),
            dma((strips,)),
            dma((n_x, strips)),
            dma((n_x, strips)),
            dma((n_x, strips)),
            dma((n_x, strips)),
            dma((strips,)),
            dma((strips,)),
        ],
        compiler_params=pltpu.CompilerParams(
            collective_id=0, has_side_effects=True, vmem_limit_bytes=56 * 2**20
        ),
        cost_estimate=pl.CostEstimate(
            flops=flops, bytes_accessed=3 * ri * rows * n_v * 2, transcendentals=0
        ),
    )(
        amps.reshape(ri, rows, n_v),
        integrals.reshape(ri, rows, n_v),
        ladder_ints,
        eps_occ,
        eps_vir.reshape(1, n_v),
        pair_mask,
    )
    return new.reshape(ri, nb, n_o, n_v), energy


def solution(mesh):
    in_specs = (
        P(("groups", "occ"), "vir", None, None),
        P(("groups", "occ"), "vir", None, None),
        P(("groups", "occ"), None, None, None),
        P("groups"),
        P("groups"),
        P(("groups", "occ"), None),
    )
    out_specs = (P(("groups", "occ"), "vir", None, None), P(("groups", "occ"), None))
    body = functools.partial(per_device, mesh.shape["occ"], mesh.shape["vir"])
    return jax.shard_map(
        body, mesh=mesh, in_specs=in_specs, out_specs=out_specs, check_vma=False
    )
```

```python
import functools

import jax
import jax.numpy as jnp
from jax import lax
from jax.experimental import pallas as pl
from jax.experimental.pallas import tpu as pltpu
from jax.sharding import PartitionSpec as P

F32, BF16 = jnp.float32, jnp.bfloat16
MESH = pl.DeviceIdType.MESH
TILE = 256
LANES = 128
K_PARTS = 2


def iota(shape, axis):
    return lax.broadcasted_iota(jnp.int32, shape, axis)


def dot(left, right):
    return jnp.dot(left, right, preferred_element_type=F32)


def kernel(
    n_occ, n_vir, nb, n_o,
    a_hbm, g_hbm, w_ref, eo_ref, ev_ref, mask_ref,
    new_ref, en_ref,
    amps, panel, direct, wblk, acc, rden, eall,
    load_sem, z_send, z_recv, x_send, x_recv, c_send, c_recv, e_send, e_recv,
):
    ri, rows, n_v = g_hbm.shape
    n_x = n_occ // 2
    tiles = rows // TILE
    k_per = n_o // K_PARTS
    o_bits = n_o.bit_length() - 1
    chunks = [(i, h) for i in range(ri) for h in range(K_PARTS)]

    z = lax.axis_index("vir")
    m = lax.axis_index("occ")
    sib = m + 1 - 2 * lax.rem(m, 2)
    x_right = lax.rem(m + 2, n_occ)
    x_left = lax.rem(m + n_occ - 2, n_occ)

    def amps_block(origin):
        return amps.at[pl.ds(origin * ri, ri)]

    load_g = [
        pltpu.make_async_copy(g_hbm.at[i], direct.at[i], load_sem.at[i]) for i in range(ri)
    ]
    load_a = pltpu.make_async_copy(a_hbm, amps_block(m), load_sem.at[ri])
    for copy in load_g:
        copy.start()
    load_a.start()

    barrier = pltpu.get_barrier_semaphore()
    for d in range(1, n_vir):
        pl.semaphore_signal(
            barrier, inc=1, device_id={"vir": lax.rem(z + d, n_vir)}, device_id_type=MESH
        )
    for peer in (sib, x_right, x_left):
        pl.semaphore_signal(barrier, inc=1, device_id={"occ": peer}, device_id_type=MESH)

    c_sub = max(TILE // n_o, 16)
    part = c_sub * n_o
    sub_bits = c_sub.bit_length() - 1
    to_row = iota((part, part), 0)
    source = ((to_row & (c_sub - 1)) << o_bits) + (to_row >> sub_bits)
    shuffle = jnp.where(iota((part, part), 1) == source, 1.0, 0.0).astype(BF16)

    def permute(i):
        for s in range(nb // c_sub):
            block = dot(shuffle, direct[i, pl.ds(s * part, part), :]).astype(BF16)
            first = pl.multiple_of(z * nb + s * c_sub, c_sub)
            panel[i, :, pl.ds(first, c_sub), :] = block.reshape(n_o, c_sub, n_v)

    def z_copy(way, origin, q):
        i, h = chunks[q]
        first = pl.multiple_of(origin * nb, nb)
        block = panel.at[i, pl.ds(h * k_per, k_per), pl.ds(first, nb), :]
        target = jnp.clip(z + (1 if way == 0 else -1), 0, n_vir - 1)
        return pltpu.make_async_remote_copy(
            src_ref=block,
            dst_ref=block,
            send_sem=z_send.at[way, origin, q],
            recv_sem=z_recv.at[way, origin, q],
            device_id={"vir": target},
            device_id_type=MESH,
        )

    def has_next(way):
        return z < n_vir - 1 if way == 0 else z > 0

    def origin_of(way, step):
        return z - step if way == 0 else z + step

    def exists(way, step):
        return z - step >= 0 if way == 0 else z + step < n_vir

    def z_start(way, origin, q):
        z_copy(way, origin, q).start()

    def x_copy(step, source=None):
        origin = lax.rem(m + n_occ - 2 * step, n_occ)
        return pltpu.make_async_remote_copy(
            src_ref=amps_block(origin) if source is None else source,
            dst_ref=amps_block(origin),
            send_sem=x_send.at[step],
            recv_sem=x_recv.at[step],
            device_id={"occ": x_right},
            device_id_type=MESH,
        )

    def c_copy(step, source=None):
        origin = lax.rem(m + n_occ - 2 * step, n_occ)
        return pltpu.make_async_remote_copy(
            src_ref=amps_block(origin) if source is None else source,
            dst_ref=amps_block(origin),
            send_sem=c_send.at[step],
            recv_sem=c_recv.at[step],
            device_id={"occ": sib},
            device_id_type=MESH,
        )

    def e_copy(d, i):
        return pltpu.make_async_remote_copy(
            src_ref=eall.at[z, i],
            dst_ref=eall.at[z, i],
            send_sem=e_send.at[d, i],
            recv_sem=e_recv.at[d, i],
            device_id={"vir": lax.rem(z + d, n_vir)},
            device_id_type=MESH,
        )

    def e_arrival(d, i):
        origin = lax.rem(z + n_vir - d, n_vir)
        return pltpu.make_async_remote_copy(
            src_ref=eall.at[origin, i],
            dst_ref=eall.at[origin, i],
            send_sem=e_send.at[d, i],
            recv_sem=e_recv.at[d, i],
            device_id={"vir": origin},
            device_id_type=MESH,
        )

    load_g[0].wait()
    permute(0)
    pl.semaphore_wait(barrier, n_vir + 2)
    for i in range(ri):
        if i:
            load_g[i].wait()
            permute(i)
        for q, (qi, _) in enumerate(chunks):
            if qi == i:
                for way in (0, 1):
                    pl.when(has_next(way))(functools.partial(z_start, way, z, q))
        if i == 0:
            load_a.wait()
            if n_x > 1:
                x_copy(0).start()
            c_copy(0).start()

    row = iota((TILE, 1), 0)
    row_j = row & (n_o - 1)
    eps_j = jnp.zeros((TILE, 1), F32)
    keep = [jnp.zeros((TILE, 1), F32) for _ in range(ri)]
    for j in range(n_o):
        eps_j = jnp.where(row_j == j, eo_ref[j], eps_j)
        for i in range(ri):
            keep[i] = jnp.where(row_j == j, mask_ref[i, j].astype(F32), keep[i])
    ev = ev_ref[...]

    def factors(t, carry):
        own = iota((TILE, n_v), 1) == z * nb + ((t * TILE + iota((TILE, n_v), 0)) >> o_bits)
        eps_b = jnp.sum(jnp.where(own, ev, 0.0), axis=1, keepdims=True)
        for i in range(ri):
            denom = ((ev + eps_b) - eo_ref[m * ri + i]) - eps_j
            rden[i, pl.ds(pl.multiple_of(t * TILE, TILE), TILE), :] = -keep[i] / denom
        return carry

    lax.fori_loop(0, tiles, factors, 0)

    up = jnp.where((iota((TILE, n_o), 0) & (n_o - 1)) == iota((TILE, n_o), 1), 1.0, 0.0)
    across = jnp.where((iota((n_o, TILE), 1) & (n_o - 1)) == iota((n_o, TILE), 0), 1.0, 0.0)
    same_b = (iota((TILE, TILE), 0) >> o_bits) == (iota((TILE, TILE), 1) >> o_bits)
    for i in range(ri):
        w_i = w_ref[i].astype(F32)

        def spread(k, carry, i=i, w_i=w_i):
            w_k = jnp.sum(jnp.where(iota(w_i.shape, 1) == k, w_i, 0.0), axis=1)
            full = dot(up, dot(w_k, across))
            wblk[i, k] = jnp.where(same_b, full, 0.0).astype(BF16)
            return carry

        lax.fori_loop(0, n_o, spread, 0)

    def forward(step, q):
        for way in (0, 1):

            def take(way=way):
                z_copy(way, origin_of(way, step), q).wait_recv()
                pl.when(has_next(way))(
                    functools.partial(z_start, way, origin_of(way, step), q)
                )

            pl.when(exists(way, step))(take)

    def rows_of(t):
        return pl.ds(pl.multiple_of(t * TILE, TILE), TILE)

    def ladder(i):
        def body(t, carry):
            value = direct[i, rows_of(t), :].astype(F32)

            def add(k8, value):
                for kk in range(8):
                    k = k8 * 8 + kk
                    value = value + dot(wblk[i, k], amps[k, rows_of(t), :])
                return value

            acc[i, rows_of(t), :] = lax.fori_loop(0, n_o // 8, add, value)
            return carry

        lax.fori_loop(0, tiles, body, 0)

    def cycle(q, last):
        i, h = chunks[q]

        def body(t, carry):
            value = acc[i, rows_of(t), :]

            def add(k4, value):
                for kk in range(4):
                    k = h * k_per + k4 * 4 + kk
                    value = value + dot(amps[k, rows_of(t), :], panel[i, k])
                return value

            value = lax.fori_loop(0, k_per // 4, add, value)
            if not last:
                acc[i, rows_of(t), :] = value
                return carry
            new = (value * rden[i, rows_of(t), :]).astype(BF16)
            new_ref[i, rows_of(t), :] = new
            prod = direct[i, rows_of(t), :].astype(F32) * new.astype(F32)
            return carry + jnp.sum(prod.reshape(TILE // n_o, n_o, n_v), axis=0)

        if not last:
            lax.fori_loop(0, tiles, body, 0)
            return
        energy = lax.fori_loop(0, tiles, body, jnp.zeros((n_o, n_v), F32))
        folded = energy[:, :LANES]
        for s in range(1, n_v // LANES):
            folded = folded + energy[:, s * LANES : (s + 1) * LANES]
        eall[z, i] = folded
        for d in range(1, n_vir):
            e_copy(d, i).start()

    def amps_step(step):
        if step:
            x_copy(step - 1).wait_recv()
            if step < n_x - 1:
                x_copy(step).start()
            c_copy(step).start()

    work = [functools.partial(amps_step, s) for s in range(1, n_x)]

    def all_amps():
        for s in range(n_x):
            c_copy(s).wait_recv()

    tail_work = [all_amps] + [functools.partial(ladder, i) for i in range(ri)]
    slots = []
    for step in range(1, n_vir - 1):
        for q in range(len(chunks)):
            slots.append((step, q))
    for index, (step, q) in enumerate(slots):
        forward(step, q)
        if work:
            work.pop(0)()
        elif index >= len(chunks) and tail_work:
            tail_work.pop(0)()
    for piece in work + tail_work:
        piece()
    for q, (i, h) in enumerate(chunks):
        forward(n_vir - 1, q)
        cycle(q, h == K_PARTS - 1)

    for i in range(ri):
        for d in range(1, n_vir):
            e_arrival(d, i).wait_recv()
        total = eall[0, i]
        for s in range(1, n_vir):
            total = total + eall[s, i]
        column = jnp.sum(total, axis=1, keepdims=True) / n_v
        spot = iota((n_o, LANES), 0) == iota((n_o, LANES), 1)
        line = jnp.sum(jnp.where(spot, column, 0.0), axis=0, keepdims=True)
        en_ref[pl.ds(i, 1), :] = line[:, :n_o]

    for way in (0, 1):
        for step in range(n_vir):
            for q in range(len(chunks)):

                def sent(way=way, step=step, q=q):
                    z_copy(way, origin_of(way, step), q).wait_send()

                pl.when(jnp.logical_and(has_next(way), exists(way, step)))(sent)
    for s in range(n_x):
        if s < n_x - 1:
            x_copy(s).wait_send()
        c_copy(s).wait_send()
    for i in range(ri):
        for d in range(1, n_vir):
            e_copy(d, i).wait_send()


def per_device(n_occ, n_vir, amps, integrals, ladder_ints, eps_occ, eps_vir, pair_mask):
    ri, nb, n_o, n_v = amps.shape
    rows = nb * n_o
    n_chunks = ri * K_PARTS
    n_x = n_occ // 2
    flops = 2 * 2 * ri * rows * n_v * n_o * n_v
    dma = pltpu.SemaphoreType.DMA
    new, energy = pl.pallas_call(
        functools.partial(kernel, n_occ, n_vir, nb, n_o),
        out_shape=(
            pltpu.VMEM((ri, rows, n_v), BF16),
            pltpu.VMEM((ri, n_o), F32),
        ),
        in_specs=[
            pl.BlockSpec(memory_space=pl.ANY),
            pl.BlockSpec(memory_space=pl.ANY),
            pl.BlockSpec(memory_space=pltpu.VMEM),
            pl.BlockSpec(memory_space=pltpu.SMEM),
            pl.BlockSpec(memory_space=pltpu.VMEM),
            pl.BlockSpec(memory_space=pltpu.SMEM),
        ],
        out_specs=(
            pl.BlockSpec(memory_space=pltpu.VMEM),
            pl.BlockSpec(memory_space=pltpu.VMEM),
        ),
        scratch_shapes=[
            pltpu.VMEM((n_o, rows, n_v), BF16),
            pltpu.VMEM((ri, n_o, n_v, n_v), BF16),
            pltpu.VMEM((ri, rows, n_v), BF16),
            pltpu.VMEM((ri, n_o, TILE, TILE), BF16),
            pltpu.VMEM((ri, rows, n_v), F32),
            pltpu.VMEM((ri, rows, n_v), F32),
            pltpu.VMEM((n_vir, ri, n_o, LANES), F32),
            dma((ri + 1,)),
            dma((2, n_vir, n_chunks)),
            dma((2, n_vir, n_chunks)),
            dma((n_x,)),
            dma((n_x,)),
            dma((n_x,)),
            dma((n_x,)),
            dma((n_vir, ri)),
            dma((n_vir, ri)),
        ],
        compiler_params=pltpu.CompilerParams(
            collective_id=0, has_side_effects=True, vmem_limit_bytes=56 * 2**20
        ),
        cost_estimate=pl.CostEstimate(
            flops=flops, bytes_accessed=3 * ri * rows * n_v * 2, transcendentals=0
        ),
    )(
        amps.reshape(ri, rows, n_v),
        integrals.reshape(ri, rows, n_v),
        ladder_ints,
        eps_occ,
        eps_vir.reshape(1, n_v),
        pair_mask,
    )
    return new.reshape(ri, nb, n_o, n_v), energy


def solution(mesh):
    in_specs = (
        P(("groups", "occ"), "vir", None, None),
        P(("groups", "occ"), "vir", None, None),
        P(("groups", "occ"), None, None, None),
        P("groups"),
        P("groups"),
        P(("groups", "occ"), None),
    )
    out_specs = (P(("groups", "occ"), "vir", None, None), P(("groups", "occ"), None))
    body = functools.partial(per_device, mesh.shape["occ"], mesh.shape["vir"])
    return jax.shard_map(
        body, mesh=mesh, in_specs=in_specs, out_specs=out_specs, check_vma=False
    )
```

```python
import functools

import jax
import jax.numpy as jnp
from jax import lax
from jax.experimental import pallas as pl
from jax.experimental.pallas import tpu as pltpu
from jax.sharding import PartitionSpec as P

F32, BF16 = jnp.float32, jnp.bfloat16
MESH = pl.DeviceIdType.MESH
TILE = 256
LANES = 128
K_PARTS = 4


def iota(shape, axis):
    return lax.broadcasted_iota(jnp.int32, shape, axis)


def dot(left, right):
    return jnp.dot(left, right, preferred_element_type=F32)


def kernel(
    n_occ, n_vir, nb, n_o,
    a_hbm, g_hbm, w_ref, eo_ref, ev_ref, mask_ref,
    new_ref, en_ref,
    amps, panel, direct, wblk, acc, rden, eall,
    load_sem, z_send, z_recv, x_send, x_recv, c_send, c_recv, e_send, e_recv,
):
    ri, rows, n_v = g_hbm.shape
    n_x = n_occ // 2
    tiles = rows // TILE
    k_per = n_o // K_PARTS
    group = min(4, k_per)
    o_bits = n_o.bit_length() - 1
    chunks = [(i, h) for i in range(ri) for h in range(K_PARTS)]

    z = lax.axis_index("vir")
    m = lax.axis_index("occ")
    sib = m + 1 - 2 * lax.rem(m, 2)
    x_right = lax.rem(m + 2, n_occ)
    x_left = lax.rem(m + n_occ - 2, n_occ)

    def amps_block(origin):
        return amps.at[pl.ds(origin * ri, ri)]

    load_g = [
        pltpu.make_async_copy(g_hbm.at[i], direct.at[i], load_sem.at[i]) for i in range(ri)
    ]
    load_a = pltpu.make_async_copy(a_hbm, amps_block(m), load_sem.at[ri])
    for copy in load_g:
        copy.start()
    load_a.start()

    barrier = pltpu.get_barrier_semaphore()
    for d in range(1, n_vir):
        pl.semaphore_signal(
            barrier, inc=1, device_id={"vir": lax.rem(z + d, n_vir)}, device_id_type=MESH
        )
    for peer in (sib, x_right, x_left):
        pl.semaphore_signal(barrier, inc=1, device_id={"occ": peer}, device_id_type=MESH)

    c_sub = max(TILE // n_o, 16)
    part = c_sub * n_o
    sub_bits = c_sub.bit_length() - 1
    to_row = iota((part, part), 0)
    source = ((to_row & (c_sub - 1)) << o_bits) + (to_row >> sub_bits)
    shuffle = jnp.where(iota((part, part), 1) == source, 1.0, 0.0).astype(BF16)

    def permute(i):
        for s in range(nb // c_sub):
            block = dot(shuffle, direct[i, pl.ds(s * part, part), :]).astype(BF16)
            first = pl.multiple_of(z * nb + s * c_sub, c_sub)
            panel[i, :, pl.ds(first, c_sub), :] = block.reshape(n_o, c_sub, n_v)

    def z_copy(way, origin, q):
        i, h = chunks[q]
        first = pl.multiple_of(origin * nb, nb)
        block = panel.at[i, pl.ds(h * k_per, k_per), pl.ds(first, nb), :]
        target = jnp.clip(z + (1 if way == 0 else -1), 0, n_vir - 1)
        return pltpu.make_async_remote_copy(
            src_ref=block,
            dst_ref=block,
            send_sem=z_send.at[way, origin, q],
            recv_sem=z_recv.at[way, origin, q],
            device_id={"vir": target},
            device_id_type=MESH,
        )

    def has_next(way):
        return z < n_vir - 1 if way == 0 else z > 0

    def origin_of(way, step):
        return z - step if way == 0 else z + step

    def exists(way, step):
        return z - step >= 0 if way == 0 else z + step < n_vir

    def z_start(way, origin, q):
        z_copy(way, origin, q).start()

    def x_copy(step, source=None):
        origin = lax.rem(m + n_occ - 2 * step, n_occ)
        return pltpu.make_async_remote_copy(
            src_ref=amps_block(origin) if source is None else source,
            dst_ref=amps_block(origin),
            send_sem=x_send.at[step],
            recv_sem=x_recv.at[step],
            device_id={"occ": x_right},
            device_id_type=MESH,
        )

    def c_copy(step, source=None):
        origin = lax.rem(m + n_occ - 2 * step, n_occ)
        return pltpu.make_async_remote_copy(
            src_ref=amps_block(origin) if source is None else source,
            dst_ref=amps_block(origin),
            send_sem=c_send.at[step],
            recv_sem=c_recv.at[step],
            device_id={"occ": sib},
            device_id_type=MESH,
        )

    def e_copy(d, i):
        return pltpu.make_async_remote_copy(
            src_ref=eall.at[z, i],
            dst_ref=eall.at[z, i],
            send_sem=e_send.at[d, i],
            recv_sem=e_recv.at[d, i],
            device_id={"vir": lax.rem(z + d, n_vir)},
            device_id_type=MESH,
        )

    def e_arrival(d, i):
        origin = lax.rem(z + n_vir - d, n_vir)
        return pltpu.make_async_remote_copy(
            src_ref=eall.at[origin, i],
            dst_ref=eall.at[origin, i],
            send_sem=e_send.at[d, i],
            recv_sem=e_recv.at[d, i],
            device_id={"vir": origin},
            device_id_type=MESH,
        )

    load_g[0].wait()
    permute(0)
    pl.semaphore_wait(barrier, n_vir + 2)
    for i in range(ri):
        if i:
            load_g[i].wait()
            permute(i)
        for q, (qi, _) in enumerate(chunks):
            if qi == i:
                for way in (0, 1):
                    pl.when(has_next(way))(functools.partial(z_start, way, z, q))
        if i == 0:
            load_a.wait()
            if n_x > 1:
                x_copy(0).start()
            c_copy(0).start()

    row = iota((TILE, 1), 0)
    row_j = row & (n_o - 1)
    eps_j = jnp.zeros((TILE, 1), F32)
    keep = [jnp.zeros((TILE, 1), F32) for _ in range(ri)]
    for j in range(n_o):
        eps_j = jnp.where(row_j == j, eo_ref[j], eps_j)
        for i in range(ri):
            keep[i] = jnp.where(row_j == j, mask_ref[i, j].astype(F32), keep[i])
    ev = ev_ref[...]

    def factors(t, carry):
        own = iota((TILE, n_v), 1) == z * nb + ((t * TILE + iota((TILE, n_v), 0)) >> o_bits)
        eps_b = jnp.sum(jnp.where(own, ev, 0.0), axis=1, keepdims=True)
        for i in range(ri):
            denom = ((ev + eps_b) - eo_ref[m * ri + i]) - eps_j
            rden[i, pl.ds(pl.multiple_of(t * TILE, TILE), TILE), :] = -keep[i] / denom
        return carry

    lax.fori_loop(0, tiles, factors, 0)

    up = jnp.where((iota((TILE, n_o), 0) & (n_o - 1)) == iota((TILE, n_o), 1), 1.0, 0.0)
    across = jnp.where((iota((n_o, TILE), 1) & (n_o - 1)) == iota((n_o, TILE), 0), 1.0, 0.0)
    same_b = (iota((TILE, TILE), 0) >> o_bits) == (iota((TILE, TILE), 1) >> o_bits)
    for i in range(ri):
        w_i = w_ref[i].astype(F32)

        def spread(k, carry, i=i, w_i=w_i):
            w_k = jnp.sum(jnp.where(iota(w_i.shape, 1) == k, w_i, 0.0), axis=1)
            full = dot(up, dot(w_k, across))
            wblk[i, k] = jnp.where(same_b, full, 0.0).astype(BF16)
            return carry

        lax.fori_loop(0, n_o, spread, 0)

    def forward(step, q):
        for way in (0, 1):

            def take(way=way):
                z_copy(way, origin_of(way, step), q).wait_recv()
                pl.when(has_next(way))(
                    functools.partial(z_start, way, origin_of(way, step), q)
                )

            pl.when(exists(way, step))(take)

    def rows_of(t):
        return pl.ds(pl.multiple_of(t * TILE, TILE), TILE)

    def ladder(i):
        def body(t, carry):
            value = direct[i, rows_of(t), :].astype(F32)

            def add(k8, value):
                for kk in range(8):
                    k = k8 * 8 + kk
                    value = value + dot(wblk[i, k], amps[k, rows_of(t), :])
                return value

            acc[i, rows_of(t), :] = lax.fori_loop(0, n_o // 8, add, value)
            return carry

        lax.fori_loop(0, tiles, body, 0)

    def cycle(q, last):
        i, h = chunks[q]

        def body(t, carry):
            value = acc[i, rows_of(t), :]

            def add(g, value):
                for kk in range(group):
                    k = h * k_per + g * group + kk
                    value = value + dot(amps[k, rows_of(t), :], panel[i, k])
                return value

            value = lax.fori_loop(0, k_per // group, add, value)
            if not last:
                acc[i, rows_of(t), :] = value
                return carry
            new = (value * rden[i, rows_of(t), :]).astype(BF16)
            new_ref[i, rows_of(t), :] = new
            prod = direct[i, rows_of(t), :].astype(F32) * new.astype(F32)
            return carry + jnp.sum(prod.reshape(TILE // n_o, n_o, n_v), axis=0)

        if not last:
            lax.fori_loop(0, tiles, body, 0)
            return
        energy = lax.fori_loop(0, tiles, body, jnp.zeros((n_o, n_v), F32))
        folded = energy[:, :LANES]
        for s in range(1, n_v // LANES):
            folded = folded + energy[:, s * LANES : (s + 1) * LANES]
        eall[z, i] = folded
        for d in range(1, n_vir):
            e_copy(d, i).start()

    def amps_step(step):
        if step:
            x_copy(step - 1).wait_recv()
            if step < n_x - 1:
                x_copy(step).start()
            c_copy(step).start()

    work = [functools.partial(amps_step, s) for s in range(1, n_x)]

    def all_amps():
        for s in range(n_x):
            c_copy(s).wait_recv()

    tail_work = [all_amps] + [functools.partial(ladder, i) for i in range(ri)]
    slots = []
    for step in range(1, n_vir - 1):
        for q in range(len(chunks)):
            slots.append((step, q))
    for index, (step, q) in enumerate(slots):
        forward(step, q)
        if work:
            work.pop(0)()
        elif index >= len(chunks) and tail_work:
            tail_work.pop(0)()
    for piece in work + tail_work:
        piece()
    for q, (i, h) in enumerate(chunks):
        forward(n_vir - 1, q)
        cycle(q, h == K_PARTS - 1)

    for i in range(ri):
        for d in range(1, n_vir):
            e_arrival(d, i).wait_recv()
        total = eall[0, i]
        for s in range(1, n_vir):
            total = total + eall[s, i]
        column = jnp.sum(total, axis=1, keepdims=True) / n_v
        spot = iota((n_o, LANES), 0) == iota((n_o, LANES), 1)
        line = jnp.sum(jnp.where(spot, column, 0.0), axis=0, keepdims=True)
        en_ref[pl.ds(i, 1), :] = line[:, :n_o]

    for way in (0, 1):
        for step in range(n_vir):
            for q in range(len(chunks)):

                def sent(way=way, step=step, q=q):
                    z_copy(way, origin_of(way, step), q).wait_send()

                pl.when(jnp.logical_and(has_next(way), exists(way, step)))(sent)
    for s in range(n_x):
        if s < n_x - 1:
            x_copy(s).wait_send()
        c_copy(s).wait_send()
    for i in range(ri):
        for d in range(1, n_vir):
            e_copy(d, i).wait_send()


def per_device(n_occ, n_vir, amps, integrals, ladder_ints, eps_occ, eps_vir, pair_mask):
    ri, nb, n_o, n_v = amps.shape
    rows = nb * n_o
    n_chunks = ri * K_PARTS
    n_x = n_occ // 2
    flops = 2 * 2 * ri * rows * n_v * n_o * n_v
    dma = pltpu.SemaphoreType.DMA
    new, energy = pl.pallas_call(
        functools.partial(kernel, n_occ, n_vir, nb, n_o),
        out_shape=(
            pltpu.VMEM((ri, rows, n_v), BF16),
            pltpu.VMEM((ri, n_o), F32),
        ),
        in_specs=[
            pl.BlockSpec(memory_space=pl.ANY),
            pl.BlockSpec(memory_space=pl.ANY),
            pl.BlockSpec(memory_space=pltpu.VMEM),
            pl.BlockSpec(memory_space=pltpu.SMEM),
            pl.BlockSpec(memory_space=pltpu.VMEM),
            pl.BlockSpec(memory_space=pltpu.SMEM),
        ],
        out_specs=(
            pl.BlockSpec(memory_space=pltpu.VMEM),
            pl.BlockSpec(memory_space=pltpu.VMEM),
        ),
        scratch_shapes=[
            pltpu.VMEM((n_o, rows, n_v), BF16),
            pltpu.VMEM((ri, n_o, n_v, n_v), BF16),
            pltpu.VMEM((ri, rows, n_v), BF16),
            pltpu.VMEM((ri, n_o, TILE, TILE), BF16),
            pltpu.VMEM((ri, rows, n_v), F32),
            pltpu.VMEM((ri, rows, n_v), F32),
            pltpu.VMEM((n_vir, ri, n_o, LANES), F32),
            dma((ri + 1,)),
            dma((2, n_vir, n_chunks)),
            dma((2, n_vir, n_chunks)),
            dma((n_x,)),
            dma((n_x,)),
            dma((n_x,)),
            dma((n_x,)),
            dma((n_vir, ri)),
            dma((n_vir, ri)),
        ],
        compiler_params=pltpu.CompilerParams(
            collective_id=0, has_side_effects=True, vmem_limit_bytes=56 * 2**20
        ),
        cost_estimate=pl.CostEstimate(
            flops=flops, bytes_accessed=3 * ri * rows * n_v * 2, transcendentals=0
        ),
    )(
        amps.reshape(ri, rows, n_v),
        integrals.reshape(ri, rows, n_v),
        ladder_ints,
        eps_occ,
        eps_vir.reshape(1, n_v),
        pair_mask,
    )
    return new.reshape(ri, nb, n_o, n_v), energy


def solution(mesh):
    in_specs = (
        P(("groups", "occ"), "vir", None, None),
        P(("groups", "occ"), "vir", None, None),
        P(("groups", "occ"), None, None, None),
        P("groups"),
        P("groups"),
        P(("groups", "occ"), None),
    )
    out_specs = (P(("groups", "occ"), "vir", None, None), P(("groups", "occ"), None))
    body = functools.partial(per_device, mesh.shape["occ"], mesh.shape["vir"])
    return jax.shard_map(
        body, mesh=mesh, in_specs=in_specs, out_specs=out_specs, check_vma=False
    )
```
